32 devices in a mesh: ens: 2 (over x), lat: 16 (over z, y, core).
Axes of the slice: x: 2, y: 2, z: 4, core: 2. Of those that a mesh axis runs over, the one named last changes fastest.
Arguments:
- cot_next: float32 [6, 10, 64, 4320], P('ens', None, 'lat'), parts along dimension 0, may hold values from -6 to 6
- cot_surface: float32 [128, 4320], P(('ens', 'lat')), parts along dimension 0, may hold values from -4 to 4
- stencil: float32 [5, 64, 4320], P(None, 'lat'), may hold values from 0.1 to 0.5
- mix: float32 [9, 64, 4320], P(None, 'lat'), may hold values from 0.1 to 10
- weights: float32 [3, 10], replicated, may hold values from 0.2 to 1
- depth: float32 [64, 4320], P('lat'), may hold values from 0.5 to 6
- surface_mass: float32 [64, 4320], P('lat'), may hold values from 0.005 to 0.05
- ocean: int32 [64, 4320], P('lat'), may hold values 0 or 1
- fold_sign: int32 [3, 10], replicated, may hold values from 0 to 1
Outputs:
- cot_state: float32 [6, 10, 64, 4320], P('ens', None, 'lat'), parts along dimension 0
- surface_adjoint: float32 [128, 4320], P(('ens', 'lat')), parts along dimension 0
The draws below stay inside these ranges and needn't reach their ends.
There are 2 independent parts, one for each index of `ens`. The reference program is written for one: setup_inputs(seed, part) draws one part's arguments, and reference() takes and returns one part's arrays. A program takes and returns all parts, laid end to end along the dimension named above; an argument that names none is the same for every part. Nothing has to cross between parts.
All inputs are finite; a program needn't handle non-finite values. No bound on the sum of `ocean` on one device may be relied on, other than what follows from the above.
Results may differ from the reference program's by a relative error of at most 0.0003.
Values sent between devices are 32-bit elements; how exact they have to be, the bound alone decides.
A program may use at most 128 MiB of HBM per device.

```python
import math
import jax
import jax.numpy as jnp

VARS = 3
LEV = 10
NX = 4320
ITERS = 10
NY = 64


def draw_depth(key, part):
    key = jax.random.fold_in(key, 11)
    raw = jax.random.uniform(key, (NY, NX), jnp.float32)
    rough = jnp.exp(math.log(0.5) + raw * math.log(4.0))
    rise = 1.0 + 2.0 * jnp.arange(NY, dtype=jnp.float32)[:, None] / max(NY - 1, 1)
    return rough * rise


def draw_cot_surface(key, part):
    key = jax.random.fold_in(key, 23)
    return jnp.clip(jax.random.normal(key, (NY, NX), jnp.float32), -4.0, 4.0)


def set_ends(drawn, key, low, high):
    spot = [jax.random.randint(jax.random.fold_in(key, axis), (), 0, length) for axis, length in enumerate(drawn.shape)]
    widest = drawn.shape.index(max(drawn.shape))
    neighbour = spot[:widest] + [(spot[widest] + 1) % drawn.shape[widest]] + spot[widest + 1:]
    return drawn.at[tuple(spot)].set(low).at[tuple(neighbour)].set(high)


def shard_levels(key, extent, pieces, least, top_value):
    level = 1.0
    for dim, shards_of in pieces:
        draws = jax.random.uniform(jax.random.fold_in(jax.random.fold_in(key, 6), dim), (shards_of,), jnp.float32, least / len(pieces), top_value / len(pieces))
        level = level * jnp.repeat(jnp.exp(draws), extent[dim] // shards_of).reshape((-1,) + (1,) * (len(extent) - 1 - dim))
    return level


def gaussian(own_key, dims, width, most, split=(), kind=jnp.bfloat16):
    drawn = jax.random.normal(own_key, dims, jnp.float32) * width
    if len(split) > 0:
        drawn = shard_levels(own_key, dims, split, -0.22, 0.18) * drawn
    return jnp.clip(drawn, min=-most, max=most).astype(kind)


def setup_inputs(seed: int = 0, part: int = 0) -> dict:
    arg_keys = jax.random.split(jax.random.key(seed), 10)
    own_keys = jax.random.split(jax.random.fold_in(arg_keys[9], part), 10)
    cot_next = gaussian(own_keys[0], (VARS, LEV, NY, NX), 1.0, 6.0, ((2, 16),), jnp.float32)
    cot_surface = draw_cot_surface(jax.random.fold_in(jax.random.fold_in(arg_keys[9], part), 71), part)
    stencil = jnp.clip(0.1 + 0.4 * jax.random.uniform(arg_keys[2], (5, NY, NX), jnp.float32) ** shard_levels(arg_keys[2], (5, NY, NX), ((1, 16),), -0.2, 0.2), 0.1, 0.5)
    mix = jnp.clip(jnp.exp(math.log(10.0) - 4.6051702 * jax.random.uniform(arg_keys[3], (LEV - 1, NY, NX), jnp.float32) ** shard_levels(arg_keys[3], (LEV - 1, NY, NX), ((1, 16),), -0.2, 0.2)), 0.1, 10.0)
    weights = jnp.clip(jax.random.uniform(arg_keys[4], (VARS, LEV), jnp.float32, 0.2, 1.0), 0.2, 1.0)
    depth = draw_depth(jax.random.fold_in(arg_keys[9], 71), part)
    surface_mass = jnp.clip(jnp.exp(math.log(0.05) - 2.3025851 * jax.random.uniform(arg_keys[6], (NY, NX), jnp.float32) ** shard_levels(arg_keys[6], (NY, NX), ((0, 16),), -0.2, 0.2)), 0.005, 0.05)
    ocean = set_ends((jax.random.randint(arg_keys[7], (NY, NX), 0, 10) < 9).astype(jnp.int32), jax.random.fold_in(arg_keys[7], 1), 0, 1)
    fold_sign = set_ends(jax.random.randint(arg_keys[8], (VARS, LEV), 0, 2), jax.random.fold_in(arg_keys[8], 1), 0, 1).astype(jnp.int32)
    return {"cot_next": cot_next, "cot_surface": cot_surface, "stencil": stencil, "mix": mix, "weights": weights, "depth": depth, "surface_mass": surface_mass, "ocean": ocean, "fold_sign": fold_sign}


def rows_above(field):
    return jnp.concatenate([field[..., 1:, :], jnp.zeros_like(field[..., :1, :])], axis=-2)


def rows_below(field):
    return jnp.concatenate([jnp.zeros_like(field[..., :1, :]), field[..., :-1, :]], axis=-2)


def surface_links(depth, wet_cells, surface_mass):
    east_link = 0.5 * (depth + jnp.roll(depth, -1, 1)) * wet_cells * jnp.roll(wet_cells, -1, 1)
    north_link = 0.5 * (depth + rows_above(depth)) * wet_cells * rows_above(wet_cells)
    south_link = rows_below(north_link)
    centre = surface_mass + east_link + jnp.roll(east_link, 1, 1) + north_link + south_link
    return east_link, north_link, south_link, centre


def surface_operator(field, links):
    east_link, north_link, south_link, centre = links
    return (centre * field - east_link * jnp.roll(field, -1, 1)
            - jnp.roll(east_link, 1, 1) * jnp.roll(field, 1, 1)
            - north_link * rows_above(field) - south_link * rows_below(field))


def column_solve(rhs, mix):
    levels = rhs.shape[1]
    ratios = []
    reduced = []
    for level in range(levels):
        below = mix[level - 1] if level > 0 else 0.0
        above = mix[level] if level < levels - 1 else 0.0
        pivot = 1.0 + below + above
        source = rhs[:, level]
        if level > 0:
            pivot = pivot + below * ratios[-1]
            source = source + below * reduced[-1]
        ratios.append(-above / pivot)
        reduced.append(source / pivot)
    result = [reduced[-1]]
    for level in range(levels - 2, -1, -1):
        result.insert(0, reduced[level] - ratios[level] * result[0])
    return jnp.stack(result, axis=1)


def reference(cot_next, cot_surface, stencil, mix, weights, depth, surface_mass, ocean, fold_sign):
    wet_cells = ocean.astype(jnp.float32)
    links = surface_links(depth, wet_cells, surface_mass)
    centre = links[3]
    residual = wet_cells * cot_surface
    surface = jnp.zeros_like(residual)
    scaled = residual / centre
    direction = scaled
    norm_now = jnp.sum(residual * scaled)
    for iteration in range(ITERS):
        applied = surface_operator(direction, links)
        step_size = norm_now / jnp.sum(direction * applied)
        surface = surface + step_size * direction
        residual = residual - step_size * applied
        scaled = residual / centre
        norm_next = jnp.sum(residual * scaled)
        direction = scaled + (norm_next / norm_now) * direction
        norm_now = norm_next
    forced = cot_next + weights[:, :, None, None] * (depth * surface)[None, None]
    mixed = column_solve(forced, mix)
    damped = wet_cells * mixed
    centre_c, west_c, east_c, south_c, north_c = stencil[0], stencil[1], stencil[2], stencil[3], stencil[4]
    total = (centre_c * damped + jnp.roll(west_c * damped, -1, -1) + jnp.roll(east_c * damped, 1, -1)
             + rows_above(south_c * damped) + rows_below(north_c * damped))
    fold_factor = (2 * fold_sign - 1).astype(jnp.float32)
    folded = fold_factor[:, :, None] * (north_c[-1, ::-1] * damped[:, :, -1, ::-1])
    total = total.at[:, :, -1, :].add(folded)
    return total, surface
```

```python
import functools

import jax
import jax.numpy as jnp
from jax import lax
from jax.experimental import pallas as pl
from jax.experimental.pallas import tpu as pltpu
from jax.sharding import PartitionSpec as P

ITERS = 10
LANES = 128
ROWS = 8
MESH = pl.DeviceIdType.MESH


def kernel(
    count, block, nx, variables, levels,
    cot_ref, surf_in, stencil_ref, mix_ref, weights_ref, depth_ref, mass_ref, ocean_ref, fold_ref,
    out_ref, surface_ref,
    gathered, pbuf, qbuf, rbuf, ebuf, nbuf, sbuf, xbuf, surface_ext, dbuf, wbuf,
    cot_ext, mix_ext, coef_ext, flipped, reverse_in,
    up_out, down_out, up_in, down_in,
    zs, zr, ys, yr, cs, cr, hs, hr,
):
    tiles = -(-nx // LANES)
    tail = nx - (tiles - 1) * LANES
    width = tiles * LANES
    depths = count // 4
    total_rows = count * block
    row_tiles = total_rows // ROWS
    fields = variables * levels

    me = lax.axis_index("lat")
    core = me % 2
    side = (me // 2) % 2
    plane = me // 4

    def index_of(z, y, c):
        return (z * 2 + y) * 2 + c

    def span(c):
        return slice(c * LANES, min(nx, (c + 1) * LANES))

    def cols(c):
        return slice(c * LANES, (c + 1) * LANES)

    def copy(src, dst, ssem, rsem, to):
        return pltpu.make_async_remote_copy(
            src_ref=src, dst_ref=dst, send_sem=ssem, recv_sem=rsem, device_id={"lat": to}, device_id_type=MESH
        )

    other_side = index_of(plane, 1 - side, core)
    other_core = index_of(plane, side, 1 - core)
    above = (me + 1) % count
    below = (me + count - 1) % count
    planes = [(plane + d) % depths for d in range(1, depths)]

    barrier = pltpu.get_barrier_semaphore()
    partners = [index_of(z, side, core) for z in planes] + [other_side, other_core, above, below]
    for partner in partners:
        pl.semaphore_signal(barrier, inc=1, device_id={"lat": partner}, device_id_type=MESH)

    wet_own = ocean_ref[...].astype(jnp.float32)
    gathered[me, 0] = depth_ref[...]
    gathered[me, 1] = wet_own
    gathered[me, 2] = mass_ref[...]
    gathered[me, 3] = wet_own * surf_in[...]
    pl.semaphore_wait(barrier, len(partners))

    sent = []

    def send(src_index, ssem, rsem, to):
        c = copy(gathered.at[src_index], gathered.at[src_index], ssem, rsem, to)
        c.start()
        sent.append(c)

    def arrived(src_index, ssem, rsem):
        copy(gathered.at[src_index], gathered.at[src_index], ssem, rsem, other_core).wait_recv()

    for z in planes:
        send(me, zs.at[z], zr.at[plane], index_of(z, side, core))
    send(me, ys.at[plane], yr.at[plane], other_side)
    send(me, cs.at[plane], cr.at[plane], other_core)

    for v in range(variables):
        for k in range(levels):
            up_out[pl.ds(v * levels + k, 1)] = cot_ref[v, k, block - 1:block, :]
            down_out[pl.ds(v * levels + k, 1)] = cot_ref[v, k, 0:1, :]
    for k in range(levels - 1):
        up_out[pl.ds(fields + k, 1)] = mix_ref[k, block - 1:block, :]
        down_out[pl.ds(fields + k, 1)] = mix_ref[k, 0:1, :]
    up_out[pl.ds(fields + levels - 1, 1)] = stencil_ref[4, block - 1:block, :]
    down_out[pl.ds(fields + levels - 1, 1)] = stencil_ref[3, 0:1, :]

    for z in planes:
        source = index_of(z, side, core)
        arrived(source, zs.at[z], zr.at[z])
        send(source, ys.at[z], yr.at[z], other_side)
        send(source, cs.at[z], cr.at[z], other_core)

    def ext_zero(ref):
        ref[:, :, (tiles - 1) * LANES:] = jnp.zeros(ref.shape[:2] + (LANES,), jnp.float32)
        ref[:, block:, :] = jnp.zeros((ref.shape[0], ROWS - block, width), jnp.float32)

    for ref in (cot_ext, mix_ext, coef_ext):
        ext_zero(ref)
    reverse_in[...] = jnp.zeros_like(reverse_in)
    damped = cot_ext
    for v in range(variables):
        cot_ext[pl.ds(v * levels, levels), 0:block, 0:nx] = cot_ref[v]
    mix_ext[:, 0:block, 0:nx] = mix_ref[...]
    coef_ext[:, 0:block, 0:nx] = stencil_ref[...]
    for ref in (pbuf, qbuf, rbuf):
        ref[:, :, (tiles - 1) * LANES:] = jnp.zeros((row_tiles + 2, ROWS, LANES), jnp.float32)
    xbuf[...] = jnp.zeros_like(xbuf)

    for z in [plane] + planes:
        source = index_of(z, 1 - side, core)
        arrived(source, ys.at[z], yr.at[z])
        send(source, cs.at[depths + z], cr.at[depths + z], other_core)

    halo_up = copy(up_out, up_in, hs.at[0], hr.at[0], above)
    halo_down = copy(down_out, down_in, hs.at[1], hr.at[1], below)
    halo_up.start()
    halo_down.start()

    for z in [plane] + planes:
        arrived(index_of(z, side, 1 - core), cs.at[z], cr.at[z])
        arrived(index_of(z, 1 - side, 1 - core), cs.at[depths + z], cr.at[depths + z])

    lane = lax.broadcasted_iota(jnp.int32, (ROWS, LANES), 1)
    sub = lax.broadcasted_iota(jnp.int32, (ROWS, LANES), 0)

    def roll(x, by):
        return pltpu.roll(x, by % LANES, 1)

    def east(get):
        first = get(0)
        now = first
        for c in range(tiles):
            if c < tiles - 1:
                after = get(c + 1)
                yield c, jnp.where(lane == LANES - 1, roll(after, -1), roll(now, -1))
                now = after
            else:
                yield c, jnp.where(lane == tail - 1, roll(first, tail - 1), roll(now, -1))

    def west(get):
        before = roll(get(tiles - 1), LANES - tail + 1)
        for c in range(tiles):
            x = get(c)
            if c == tiles - 1:
                x = jnp.where(lane < tail - 1, x, 0.0)
            rolled = roll(x, 1)
            yield c, jnp.where(lane == 0, before, rolled)
            before = rolled

    def wrap(ref):
        ref[0] = pltpu.roll(ref[row_tiles], 1, 0)
        ref[row_tiles + 1] = pltpu.roll(ref[1], ROWS - 1, 0)

    strip = row_tiles // block

    def place(t, carry, targets):
        for r in range(block):
            for field, ref in targets:
                for c in range(tiles):
                    parts = [gathered[s * strip + t, field, r:r + 1, span(c)] for s in range(ROWS)]
                    ref[t * block + r + 1, :, span(c)] = jnp.concatenate(parts, axis=0)
        return carry

    lax.fori_loop(0, strip, functools.partial(place, targets=((0, pbuf), (1, qbuf), (2, rbuf))), 0)
    wrap(pbuf)
    wrap(qbuf)

    for field, ref in ((0, dbuf), (1, wbuf)):
        ref[...] = jnp.zeros_like(ref)
        ref[0:block, 0:nx] = gathered[me, field]
        ref[block:block + 1, 0:nx] = gathered[above, field, 0:1]
        ref[ROWS - 1:ROWS, 0:nx] = gathered[below, field, block - 1:block]

    def links(t, carry):
        for (c, de), (_, we) in zip(east(lambda c: pbuf[t, :, cols(c)]), east(lambda c: qbuf[t, :, cols(c)])):
            d, w = pbuf[t, :, cols(c)], qbuf[t, :, cols(c)]
            ebuf[t, :, cols(c)] = 0.5 * (d + de) * w * we
            nbuf[t, :, cols(c)] = 0.5 * (d + pbuf[t + 1, :, cols(c)]) * w * qbuf[t + 1, :, cols(c)]
        return carry

    lax.fori_loop(1, row_tiles + 1, links, 0)
    for c in range(tiles):
        nbuf[row_tiles, :, cols(c)] = jnp.where(sub == ROWS - 1, 0.0, nbuf[row_tiles, :, cols(c)])
    wrap(nbuf)

    def scales(t, carry):
        for c, ew in west(lambda c: ebuf[t, :, cols(c)]):
            centre = rbuf[t, :, cols(c)] + ebuf[t, :, cols(c)] + ew + nbuf[t, :, cols(c)] + nbuf[t - 1, :, cols(c)]
            if c == tiles - 1:
                centre = jnp.where(lane < tail, centre, 1.0)
            qbuf[t, :, cols(c)] = 1.0 / jnp.sqrt(centre)
        return carry

    lax.fori_loop(1, row_tiles + 1, scales, 0)
    wrap(qbuf)
    lax.fori_loop(0, strip, functools.partial(place, targets=((3, rbuf),)), 0)

    def rescale(t, carry):
        for c, se in east(lambda c: qbuf[t, :, cols(c)]):
            s = qbuf[t, :, cols(c)]
            ebuf[t, :, cols(c)] = ebuf[t, :, cols(c)] * s * se
            nbuf[t, :, cols(c)] = nbuf[t, :, cols(c)] * s * qbuf[t + 1, :, cols(c)]
        return carry

    lax.fori_loop(1, row_tiles + 1, rescale, 0)
    wrap(nbuf)

    zero = jnp.zeros((ROWS, LANES), jnp.float32)

    def begin(t, acc):
        for c in range(tiles):
            r = rbuf[t, :, cols(c)] * qbuf[t, :, cols(c)]
            rbuf[t, :, cols(c)] = r
            pbuf[t, :, cols(c)] = r
            acc = acc + r * r
        return acc

    norm = jnp.sum(lax.fori_loop(1, row_tiles + 1, begin, zero))
    wrap(pbuf)
    own_tile = (me % strip) * block
    for m in range(block + 2):
        sbuf[m] = qbuf[own_tile + m]

    def iterate(_, norm):
        def apply(t, acc):
            acc = list(acc)
            for (c, pe), (_, pw) in zip(
                east(lambda c: pbuf[t, :, cols(c)]), west(lambda c: ebuf[t, :, cols(c)] * pbuf[t, :, cols(c)])
            ):
                p = pbuf[t, :, cols(c)]
                q = (p - ebuf[t, :, cols(c)] * pe - pw) - (
                    nbuf[t, :, cols(c)] * pbuf[t + 1, :, cols(c)] + nbuf[t - 1, :, cols(c)] * pbuf[t - 1, :, cols(c)]
                )
                qbuf[t, :, cols(c)] = q
                acc[c % 2] = acc[c % 2] + p * q
            return tuple(acc)

        a, b = lax.fori_loop(1, row_tiles + 1, apply, (zero, zero))
        step = norm / jnp.sum(a + b)

        def advance(m, carry):
            for c in range(tiles):
                xbuf[m, :, cols(c)] = xbuf[m, :, cols(c)] + step * pbuf[own_tile + m, :, cols(c)]
            return carry

        lax.fori_loop(0, block + 2, advance, 0)

        def residual(t, acc):
            acc = list(acc)
            for c in range(tiles):
                r = rbuf[t, :, cols(c)] - step * qbuf[t, :, cols(c)]
                rbuf[t, :, cols(c)] = r
                acc[c % 2] = acc[c % 2] + r * r
            return tuple(acc)

        a, b = lax.fori_loop(1, row_tiles + 1, residual, (zero, zero))
        new = jnp.sum(a + b)
        ratio = new / norm

        def direct(t, carry):
            for c in range(tiles):
                pbuf[t, :, cols(c)] = rbuf[t, :, cols(c)] + ratio * pbuf[t, :, cols(c)]
            return carry

        lax.fori_loop(1, row_tiles + 1, direct, 0)
        wrap(pbuf)
        return new

    lax.fori_loop(0, ITERS, iterate, norm)

    mine = jnp.where(sub == me // strip, 1.0, 0.0)
    surface_ext[...] = jnp.zeros_like(surface_ext)
    for c in range(tiles):
        for m, row in enumerate([ROWS - 1] + list(range(block + 1))):
            x = xbuf[m, :, cols(c)] * sbuf[m, :, cols(c)] * mine
            surface_ext[row:row + 1, cols(c)] = jnp.sum(x, axis=0, keepdims=True)
    surface_ref[...] = surface_ext[0:block, 0:nx]
    dbuf[...] = dbuf[...] * surface_ext[...]

    halo_up.wait()
    halo_down.wait()
    has_above = jnp.where(me < count - 1, 1.0, 0.0)
    has_below = jnp.where(me > 0, 1.0, 0.0)
    for f in range(fields):
        cot_ext[f, block:block + 1, 0:nx] = down_in[pl.ds(f, 1)]
        cot_ext[f, ROWS - 1:ROWS, 0:nx] = up_in[pl.ds(f, 1)]
    for k in range(levels - 1):
        mix_ext[k, block:block + 1, 0:nx] = down_in[pl.ds(fields + k, 1)]
        mix_ext[k, ROWS - 1:ROWS, 0:nx] = up_in[pl.ds(fields + k, 1)]
    coef_ext[3, block:block + 1, 0:nx] = down_in[pl.ds(fields + levels - 1, 1)] * has_above
    coef_ext[4, ROWS - 1:ROWS, 0:nx] = up_in[pl.ds(fields + levels - 1, 1)] * has_below

    def solve(c, carry):
        at = pl.ds(pl.multiple_of(c * LANES, LANES), LANES)
        mixes = [mix_ext[k, :, at] for k in range(levels - 1)]
        ratios, inverses = [], []
        for k in range(levels):
            under = mixes[k - 1] if k > 0 else 0.0
            over = mixes[k] if k < levels - 1 else 0.0
            pivot = 1.0 + under + over
            if k > 0:
                pivot = pivot + under * ratios[-1]
            inverse = 1.0 / pivot
            inverses.append(inverse)
            ratios.append(-over * inverse)
        lift, wet, north = dbuf[:, at], wbuf[:, at], coef_ext[4, :, at]
        for v in range(variables):
            reduced = []
            for k in range(levels):
                source = cot_ext[v * levels + k, :, at] + weights_ref[v, k] * lift
                if k > 0:
                    source = source + mixes[k - 1] * reduced[-1]
                reduced.append(source * inverses[k])
            result = reduced[-1]
            for k in range(levels - 1, -1, -1):
                if k < levels - 1:
                    result = reduced[k] - ratios[k] * result
                value = wet * result
                damped[v * levels + k, :, at] = value
                reverse_in[pl.ds(v * levels + k, 1), at] = (north * value)[block - 1:block]
        return carry

    lax.fori_loop(0, tiles, solve, 0)

    flag = jnp.where(me == count - 1, 1.0, 0.0)
    height = reverse_in.shape[0]
    a = lax.broadcasted_iota(jnp.int32, (2 * LANES, LANES), 0)
    b = lax.broadcasted_iota(jnp.int32, (2 * LANES, LANES), 1)
    permute = jnp.where(a + b == LANES + tail - 1, 1.0, 0.0)
    for c in range(tiles):
        if c < tiles - 1:
            x, m = reverse_in[:, (tiles - 2 - c) * LANES:(tiles - c) * LANES], permute
        else:
            x, m = reverse_in[:, 0:LANES], permute[LANES:]
        turned = jnp.dot(x, m, precision=lax.Precision.HIGHEST, preferred_element_type=jnp.float32)
        flipped[:, :, cols(c)] = turned[:, None, :]

    def horizontal(f, carry):
        sign = (2 * fold_ref[f // levels, f % levels] - 1).astype(jnp.float32) * flag
        for (c, pe), (_, pw) in zip(
            east(lambda c: coef_ext[1, :, cols(c)] * damped[f, :, cols(c)]),
            west(lambda c: coef_ext[2, :, cols(c)] * damped[f, :, cols(c)]),
        ):
            d = damped[f, :, cols(c)]
            value = (
                coef_ext[0, :, cols(c)] * d + pe + pw
                + pltpu.roll(coef_ext[3, :, cols(c)] * d, ROWS - 1, 0)
                + pltpu.roll(coef_ext[4, :, cols(c)] * d, 1, 0)
            )
            value = value + jnp.where(sub == block - 1, sign * flipped[f, :, cols(c)], 0.0)
            out_ref[f // levels, f % levels, :, span(c)] = value[0:block, 0:span(c).stop - span(c).start]
        return carry

    lax.fori_loop(0, fields, horizontal, 0)

    for c in sent:
        c.wait_send()


def solution(mesh):
    count = mesh.shape["lat"]
    in_specs = (
        P("ens", None, "lat", None),
        P(("ens", "lat"), None),
        P(None, "lat", None),
        P(None, "lat", None),
        P(),
        P("lat", None),
        P("lat", None),
        P("lat", None),
        P(),
    )
    out_specs = (P("ens", None, "lat", None), P(("ens", "lat"), None))

    def shards(cot_next, cot_surface, stencil, mix, weights, depth, surface_mass, ocean, fold_sign):
        variables, levels, block, nx = cot_next.shape
        width = -(-nx // LANES) * LANES
        row_tiles = count * block // ROWS
        depths = count // 4
        fields = variables * levels
        vmem = pl.BlockSpec(memory_space=pltpu.VMEM)
        smem = pl.BlockSpec(memory_space=pltpu.SMEM)
        f32 = jnp.float32
        ext = pltpu.VMEM((ROWS, width), f32)
        dma = pltpu.SemaphoreType.DMA
        return pl.pallas_call(
            functools.partial(kernel, count, block, nx, variables, levels),
            out_shape=(jax.ShapeDtypeStruct(cot_next.shape, f32), jax.ShapeDtypeStruct(cot_surface.shape, f32)),
            in_specs=[vmem, vmem, vmem, vmem, smem, vmem, vmem, vmem, smem],
            out_specs=(vmem, vmem),
            scratch_shapes=[
                pltpu.VMEM((count, 4, block, nx), f32),
                *[pltpu.VMEM((row_tiles + 2, ROWS, width), f32) for _ in range(5)],
                pltpu.VMEM((block + 2, ROWS, width), f32),
                pltpu.VMEM((block + 2, ROWS, width), f32),
                ext, ext, ext,
                pltpu.VMEM((fields, ROWS, width), f32),
                pltpu.VMEM((levels - 1, ROWS, width), f32),
                pltpu.VMEM((5, ROWS, width), f32),
                pltpu.VMEM((-(-fields // 8) * 8, 1, width), f32),
                pltpu.VMEM((-(-fields // 8) * 8, width), f32),
                *[pltpu.VMEM((fields + levels, nx), f32) for _ in range(4)],
                dma((depths,)), dma((depths,)), dma((depths,)), dma((depths,)),
                dma((2 * depths,)), dma((2 * depths,)), dma((2,)), dma((2,)),
            ],
            compiler_params=pltpu.CompilerParams(
                collective_id=0, has_side_effects=True, vmem_limit_bytes=60 * 1024 * 1024
            ),
        )(cot_next, cot_surface, stencil, mix, weights, depth, surface_mass, ocean, fold_sign)

    return jax.shard_map(shards, mesh=mesh, in_specs=in_specs, out_specs=out_specs, check_vma=False)
```

```python
import functools

import jax
import jax.numpy as jnp
from jax import lax
from jax.experimental import pallas as pl
from jax.experimental.pallas import tpu as pltpu
from jax.sharding import PartitionSpec as P

ITERS = 10
LANES = 128
ROWS = 8
MESH = pl.DeviceIdType.MESH


def kernel(
    count, block, nx, variables, levels,
    cot_ref, surf_in, stencil_ref, mix_ref, weights_ref, depth_ref, mass_ref, ocean_ref, fold_ref,
    out_ref, surface_ref,
    gathered, pbuf, qbuf, rbuf, ebuf, nbuf, sbuf, xbuf, surface_ext, dbuf, wbuf,
    cot_ext, mix_ext, coef_ext, flipped, reverse_in,
    up_out, down_out, up_in, down_in,
    zs, zr, ys, yr, cs, cr, hs, hr,
):
    tiles = -(-nx // LANES)
    tail = nx - (tiles - 1) * LANES
    width = tiles * LANES
    depths = count // 4
    total_rows = count * block
    row_tiles = total_rows // ROWS
    fields = variables * levels

    me = lax.axis_index("lat")
    core = me % 2
    side = (me // 2) % 2
    plane = me // 4

    def index_of(z, y, c):
        return (z * 2 + y) * 2 + c

    def span(c):
        return slice(c * LANES, min(nx, (c + 1) * LANES))

    def cols(c):
        return slice(c * LANES, (c + 1) * LANES)

    def copy(src, dst, ssem, rsem, to):
        return pltpu.make_async_remote_copy(
            src_ref=src, dst_ref=dst, send_sem=ssem, recv_sem=rsem, device_id={"lat": to}, device_id_type=MESH
        )

    other_side = index_of(plane, 1 - side, core)
    other_core = index_of(plane, side, 1 - core)
    above = (me + 1) % count
    below = (me + count - 1) % count
    planes = [(plane + d) % depths for d in range(1, depths)]

    barrier = pltpu.get_barrier_semaphore()
    partners = [index_of(z, side, core) for z in planes] + [other_side, other_core, above, below]
    for partner in partners:
        pl.semaphore_signal(barrier, inc=1, device_id={"lat": partner}, device_id_type=MESH)

    wet_own = ocean_ref[...].astype(jnp.float32)
    gathered[0, me] = depth_ref[...]
    gathered[1, me] = wet_own
    gathered[2, me] = mass_ref[...]
    gathered[3, me] = wet_own * surf_in[...]
    pl.semaphore_wait(barrier, len(partners))

    sent = []

    def send(field, src_index, ssem, rsem, to):
        part = gathered.at[field, src_index]
        c = copy(part, part, ssem, rsem, to)
        c.start()
        sent.append(c)

    def arrived(field, src_index, ssem, rsem):
        part = gathered.at[field, src_index]
        copy(part, part, ssem, rsem, other_core).wait_recv()

    for f in range(4):
        for z in planes:
            send(f, me, zs.at[f, z], zr.at[f, plane], index_of(z, side, core))
        send(f, me, ys.at[f, plane], yr.at[f, plane], other_side)
        send(f, me, cs.at[f, plane], cr.at[f, plane], other_core)

    for v in range(variables):
        for k in range(levels):
            up_out[pl.ds(v * levels + k, 1)] = cot_ref[v, k, block - 1:block, :]
            down_out[pl.ds(v * levels + k, 1)] = cot_ref[v, k, 0:1, :]
    for k in range(levels - 1):
        up_out[pl.ds(fields + k, 1)] = mix_ref[k, block - 1:block, :]
        down_out[pl.ds(fields + k, 1)] = mix_ref[k, 0:1, :]
    up_out[pl.ds(fields + levels - 1, 1)] = stencil_ref[4, block - 1:block, :]
    down_out[pl.ds(fields + levels - 1, 1)] = stencil_ref[3, 0:1, :]

    def ext_zero(ref):
        ref[:, :, (tiles - 1) * LANES:] = jnp.zeros(ref.shape[:2] + (LANES,), jnp.float32)
        ref[:, block:, :] = jnp.zeros((ref.shape[0], ROWS - block, width), jnp.float32)

    for ref in (cot_ext, mix_ext, coef_ext):
        ext_zero(ref)
    reverse_in[...] = jnp.zeros_like(reverse_in)
    damped = cot_ext
    for v in range(variables):
        cot_ext[pl.ds(v * levels, levels), 0:block, 0:nx] = cot_ref[v]
    mix_ext[:, 0:block, 0:nx] = mix_ref[...]
    coef_ext[:, 0:block, 0:nx] = stencil_ref[...]
    for ref in (pbuf, qbuf, rbuf):
        ref[:, :, (tiles - 1) * LANES:] = jnp.zeros((row_tiles + 2, ROWS, LANES), jnp.float32)
    xbuf[...] = jnp.zeros_like(xbuf)

    def from_planes(f):
        for z in planes:
            source = index_of(z, side, core)
            arrived(f, source, zs.at[f, z], zr.at[f, z])
            send(f, source, ys.at[f, z], yr.at[f, z], other_side)
            send(f, source, cs.at[f, z], cr.at[f, z], other_core)

    def from_side(f):
        for z in [plane] + planes:
            source = index_of(z, 1 - side, core)
            arrived(f, source, ys.at[f, z], yr.at[f, z])
            send(f, source, cs.at[f, depths + z], cr.at[f, depths + z], other_core)

    def from_core(f):
        for z in [plane] + planes:
            arrived(f, index_of(z, side, 1 - core), cs.at[f, z], cr.at[f, z])
            arrived(f, index_of(z, 1 - side, 1 - core), cs.at[f, depths + z], cr.at[f, depths + z])

    halo_up = copy(up_out, up_in, hs.at[0], hr.at[0], above)
    halo_down = copy(down_out, down_in, hs.at[1], hr.at[1], below)

    from_planes(0)
    from_planes(1)
    from_side(0)
    from_planes(2)
    from_side(1)
    from_planes(3)
    from_side(2)

    lane = lax.broadcasted_iota(jnp.int32, (ROWS, LANES), 1)
    sub = lax.broadcasted_iota(jnp.int32, (ROWS, LANES), 0)

    def roll(x, by):
        return pltpu.roll(x, by % LANES, 1)

    def east(get):
        first = get(0)
        now = first
        for c in range(tiles):
            if c < tiles - 1:
                after = get(c + 1)
                yield c, jnp.where(lane == LANES - 1, roll(after, -1), roll(now, -1))
                now = after
            else:
                yield c, jnp.where(lane == tail - 1, roll(first, tail - 1), roll(now, -1))

    def west(get):
        before = roll(get(tiles - 1), LANES - tail + 1)
        for c in range(tiles):
            x = get(c)
            if c == tiles - 1:
                x = jnp.where(lane < tail - 1, x, 0.0)
            rolled = roll(x, 1)
            yield c, jnp.where(lane == 0, before, rolled)
            before = rolled

    def wrap(ref):
        ref[0] = pltpu.roll(ref[row_tiles], 1, 0)
        ref[row_tiles + 1] = pltpu.roll(ref[1], ROWS - 1, 0)

    strip = row_tiles // block

    def place(t, carry, targets):
        for r in range(block):
            for field, ref in targets:
                for c in range(tiles):
                    parts = [gathered[field, s * strip + t, r:r + 1, span(c)] for s in range(ROWS)]
                    ref[t * block + r + 1, :, span(c)] = jnp.concatenate(parts, axis=0)
        return carry

    def place_all(field, ref):
        lax.fori_loop(0, strip, functools.partial(place, targets=((field, ref),)), 0)

    from_core(0)
    place_all(0, pbuf)
    from_core(1)
    from_side(3)
    halo_up.start()
    halo_down.start()
    place_all(1, qbuf)
    wrap(pbuf)
    wrap(qbuf)

    for field, ref in ((0, dbuf), (1, wbuf)):
        ref[...] = jnp.zeros_like(ref)
        ref[0:block, 0:nx] = gathered[field, me]
        ref[block:block + 1, 0:nx] = gathered[field, above, 0:1]
        ref[ROWS - 1:ROWS, 0:nx] = gathered[field, below, block - 1:block]

    def links(t, carry):
        for (c, de), (_, we) in zip(east(lambda c: pbuf[t, :, cols(c)]), east(lambda c: qbuf[t, :, cols(c)])):
            d, w = pbuf[t, :, cols(c)], qbuf[t, :, cols(c)]
            ebuf[t, :, cols(c)] = 0.5 * (d + de) * w * we
            nbuf[t, :, cols(c)] = 0.5 * (d + pbuf[t + 1, :, cols(c)]) * w * qbuf[t + 1, :, cols(c)]
        return carry

    lax.fori_loop(1, row_tiles + 1, links, 0)
    for c in range(tiles):
        nbuf[row_tiles, :, cols(c)] = jnp.where(sub == ROWS - 1, 0.0, nbuf[row_tiles, :, cols(c)])
    wrap(nbuf)

    from_core(2)
    place_all(2, rbuf)

    def scales(t, carry):
        for c, ew in west(lambda c: ebuf[t, :, cols(c)]):
            centre = rbuf[t, :, cols(c)] + ebuf[t, :, cols(c)] + ew + nbuf[t, :, cols(c)] + nbuf[t - 1, :, cols(c)]
            if c == tiles - 1:
                centre = jnp.where(lane < tail, centre, 1.0)
            qbuf[t, :, cols(c)] = 1.0 / jnp.sqrt(centre)
        return carry

    lax.fori_loop(1, row_tiles + 1, scales, 0)
    wrap(qbuf)
    from_core(3)
    place_all(3, rbuf)

    def rescale(t, carry):
        for c, se in east(lambda c: qbuf[t, :, cols(c)]):
            s = qbuf[t, :, cols(c)]
            ebuf[t, :, cols(c)] = ebuf[t, :, cols(c)] * s * se
            nbuf[t, :, cols(c)] = nbuf[t, :, cols(c)] * s * qbuf[t + 1, :, cols(c)]
        return carry

    lax.fori_loop(1, row_tiles + 1, rescale, 0)
    wrap(nbuf)

    zero = jnp.zeros((ROWS, LANES), jnp.float32)

    def begin(t, acc):
        for c in range(tiles):
            r = rbuf[t, :, cols(c)] * qbuf[t, :, cols(c)]
            rbuf[t, :, cols(c)] = r
            pbuf[t, :, cols(c)] = r
            acc = acc + r * r
        return acc

    norm = jnp.sum(lax.fori_loop(1, row_tiles + 1, begin, zero))
    wrap(pbuf)
    own_tile = (me % strip) * block
    for m in range(block + 2):
        sbuf[m] = qbuf[own_tile + m]

    def iterate(_, norm):
        def apply(t, acc):
            acc = list(acc)
            for (c, pe), (_, pw) in zip(
                east(lambda c: pbuf[t, :, cols(c)]), west(lambda c: ebuf[t, :, cols(c)] * pbuf[t, :, cols(c)])
            ):
                p = pbuf[t, :, cols(c)]
                q = (p - ebuf[t, :, cols(c)] * pe - pw) - (
                    nbuf[t, :, cols(c)] * pbuf[t + 1, :, cols(c)] + nbuf[t - 1, :, cols(c)] * pbuf[t - 1, :, cols(c)]
                )
                qbuf[t, :, cols(c)] = q
                acc[c % 2] = acc[c % 2] + p * q
            return tuple(acc)

        a, b = lax.fori_loop(1, row_tiles + 1, apply, (zero, zero))
        step = norm / jnp.sum(a + b)

        def advance(m, carry):
            for c in range(tiles):
                xbuf[m, :, cols(c)] = xbuf[m, :, cols(c)] + step * pbuf[own_tile + m, :, cols(c)]
            return carry

        lax.fori_loop(0, block + 2, advance, 0)

        def residual(t, acc):
            acc = list(acc)
            for c in range(tiles):
                r = rbuf[t, :, cols(c)] - step * qbuf[t, :, cols(c)]
                rbuf[t, :, cols(c)] = r
                acc[c % 2] = acc[c % 2] + r * r
            return tuple(acc)

        a, b = lax.fori_loop(1, row_tiles + 1, residual, (zero, zero))
        new = jnp.sum(a + b)
        ratio = new / norm

        def direct(t, carry):
            for c in range(tiles):
                pbuf[t, :, cols(c)] = rbuf[t, :, cols(c)] + ratio * pbuf[t, :, cols(c)]
            return carry

        lax.fori_loop(1, row_tiles + 1, direct, 0)
        wrap(pbuf)
        return new

    lax.fori_loop(0, ITERS, iterate, norm)

    mine = jnp.where(sub == me // strip, 1.0, 0.0)
    surface_ext[...] = jnp.zeros_like(surface_ext)
    for c in range(tiles):
        for m, row in enumerate([ROWS - 1] + list(range(block + 1))):
            x = xbuf[m, :, cols(c)] * sbuf[m, :, cols(c)] * mine
            surface_ext[row:row + 1, cols(c)] = jnp.sum(x, axis=0, keepdims=True)
    surface_ref[...] = surface_ext[0:block, 0:nx]
    dbuf[...] = dbuf[...] * surface_ext[...]

    halo_up.wait()
    halo_down.wait()
    has_above = jnp.where(me < count - 1, 1.0, 0.0)
    has_below = jnp.where(me > 0, 1.0, 0.0)
    for f in range(fields):
        cot_ext[f, block:block + 1, 0:nx] = down_in[pl.ds(f, 1)]
        cot_ext[f, ROWS - 1:ROWS, 0:nx] = up_in[pl.ds(f, 1)]
    for k in range(levels - 1):
        mix_ext[k, block:block + 1, 0:nx] = down_in[pl.ds(fields + k, 1)]
        mix_ext[k, ROWS - 1:ROWS, 0:nx] = up_in[pl.ds(fields + k, 1)]
    coef_ext[3, block:block + 1, 0:nx] = down_in[pl.ds(fields + levels - 1, 1)] * has_above
    coef_ext[4, ROWS - 1:ROWS, 0:nx] = up_in[pl.ds(fields + levels - 1, 1)] * has_below

    def solve(c, carry):
        at = pl.ds(pl.multiple_of(c * LANES, LANES), LANES)
        mixes = [mix_ext[k, :, at] for k in range(levels - 1)]
        ratios, inverses = [], []
        for k in range(levels):
            under = mixes[k - 1] if k > 0 else 0.0
            over = mixes[k] if k < levels - 1 else 0.0
            pivot = 1.0 + under + over
            if k > 0:
                pivot = pivot + under * ratios[-1]
            inverse = 1.0 / pivot
            inverses.append(inverse)
            ratios.append(-over * inverse)
        lift, wet, north = dbuf[:, at], wbuf[:, at], coef_ext[4, :, at]
        for v in range(variables):
            reduced = []
            for k in range(levels):
                source = cot_ext[v * levels + k, :, at] + weights_ref[v, k] * lift
                if k > 0:
                    source = source + mixes[k - 1] * reduced[-1]
                reduced.append(source * inverses[k])
            result = reduced[-1]
            for k in range(levels - 1, -1, -1):
                if k < levels - 1:
                    result = reduced[k] - ratios[k] * result
                value = wet * result
                damped[v * levels + k, :, at] = value
                reverse_in[pl.ds(v * levels + k, 1), at] = (north * value)[block - 1:block]
        return carry

    lax.fori_loop(0, tiles, solve, 0)

    flag = jnp.where(me == count - 1, 1.0, 0.0)
    height = reverse_in.shape[0]
    a = lax.broadcasted_iota(jnp.int32, (2 * LANES, LANES), 0)
    b = lax.broadcasted_iota(jnp.int32, (2 * LANES, LANES), 1)
    permute = jnp.where(a + b == LANES + tail - 1, 1.0, 0.0)
    for c in range(tiles):
        if c < tiles - 1:
            x, m = reverse_in[:, (tiles - 2 - c) * LANES:(tiles - c) * LANES], permute
        else:
            x, m = reverse_in[:, 0:LANES], permute[LANES:]
        turned = jnp.dot(x, m, precision=lax.Precision.HIGHEST, preferred_element_type=jnp.float32)
        flipped[:, :, cols(c)] = turned[:, None, :]

    def horizontal(f, carry):
        sign = (2 * fold_ref[f // levels, f % levels] - 1).astype(jnp.float32) * flag
        for (c, pe), (_, pw) in zip(
            east(lambda c: coef_ext[1, :, cols(c)] * damped[f, :, cols(c)]),
            west(lambda c: coef_ext[2, :, cols(c)] * damped[f, :, cols(c)]),
        ):
            d = damped[f, :, cols(c)]
            value = (
                coef_ext[0, :, cols(c)] * d + pe + pw
                + pltpu.roll(coef_ext[3, :, cols(c)] * d, ROWS - 1, 0)
                + pltpu.roll(coef_ext[4, :, cols(c)] * d, 1, 0)
            )
            value = value + jnp.where(sub == block - 1, sign * flipped[f, :, cols(c)], 0.0)
            out_ref[f // levels, f % levels, :, span(c)] = value[0:block, 0:span(c).stop - span(c).start]
        return carry

    lax.fori_loop(0, fields, horizontal, 0)

    for c in sent:
        c.wait_send()


def solution(mesh):
    count = mesh.shape["lat"]
    in_specs = (
        P("ens", None, "lat", None),
        P(("ens", "lat"), None),
        P(None, "lat", None),
        P(None, "lat", None),
        P(),
        P("lat", None),
        P("lat", None),
        P("lat", None),
        P(),
    )
    out_specs = (P("ens", None, "lat", None), P(("ens", "lat"), None))

    def shards(cot_next, cot_surface, stencil, mix, weights, depth, surface_mass, ocean, fold_sign):
        variables, levels, block, nx = cot_next.shape
        width = -(-nx // LANES) * LANES
        row_tiles = count * block // ROWS
        depths = count // 4
        fields = variables * levels
        vmem = pl.BlockSpec(memory_space=pltpu.VMEM)
        smem = pl.BlockSpec(memory_space=pltpu.SMEM)
        f32 = jnp.float32
        ext = pltpu.VMEM((ROWS, width), f32)
        dma = pltpu.SemaphoreType.DMA
        return pl.pallas_call(
            functools.partial(kernel, count, block, nx, variables, levels),
            out_shape=(jax.ShapeDtypeStruct(cot_next.shape, f32), jax.ShapeDtypeStruct(cot_surface.shape, f32)),
            in_specs=[vmem, vmem, vmem, vmem, smem, vmem, vmem, vmem, smem],
            out_specs=(vmem, vmem),
            scratch_shapes=[
                pltpu.VMEM((4, count, block, nx), f32),
                *[pltpu.VMEM((row_tiles + 2, ROWS, width), f32) for _ in range(5)],
                pltpu.VMEM((block + 2, ROWS, width), f32),
                pltpu.VMEM((block + 2, ROWS, width), f32),
                ext, ext, ext,
                pltpu.VMEM((fields, ROWS, width), f32),
                pltpu.VMEM((levels - 1, ROWS, width), f32),
                pltpu.VMEM((5, ROWS, width), f32),
                pltpu.VMEM((-(-fields // 8) * 8, 1, width), f32),
                pltpu.VMEM((-(-fields // 8) * 8, width), f32),
                *[pltpu.VMEM((fields + levels, nx), f32) for _ in range(4)],
                dma((4, depths)), dma((4, depths)), dma((4, depths)), dma((4, depths)),
                dma((4, 2 * depths)), dma((4, 2 * depths)), dma((2,)), dma((2,)),
            ],
            compiler_params=pltpu.CompilerParams(
                collective_id=0, has_side_effects=True, vmem_limit_bytes=60 * 1024 * 1024
            ),
        )(cot_next, cot_surface, stencil, mix, weights, depth, surface_mass, ocean, fold_sign)

    return jax.shard_map(shards, mesh=mesh, in_specs=in_specs, out_specs=out_specs, check_vma=False)
```

```python
import functools

import jax
import jax.numpy as jnp
from jax import lax
from jax.experimental import pallas as pl
from jax.experimental.pallas import tpu as pltpu
from jax.sharding import PartitionSpec as P

ITERS = 10
LANES = 128
ROWS = 8
MESH = pl.DeviceIdType.MESH


def kernel(
    members, count, block, nx, variables, levels,
    cot_ref, surf_in, stencil_ref, mix_ref, weights_ref, depth_ref, mass_ref, ocean_ref, fold_ref,
    out_ref, surface_ref,
    shared, right, pbuf, qbuf, rbuf, ebuf, nbuf, sbuf, xbuf, surface_ext, dbuf, wbuf,
    cot_ext, mix_ext, coef_ext, flipped, reverse_in,
    up_out, down_out, up_in, down_in,
    zs, zr, ys, yr, cs, cr, os, orx, xs, xr, fs, fr, hs, hr,
):
    tiles = -(-nx // LANES)
    tail = nx - (tiles - 1) * LANES
    width = tiles * LANES
    depths = count // 4
    total_rows = count * block
    row_tiles = total_rows // ROWS
    fields = variables * levels

    part_tiles = -(-tiles // members)
    part_width = part_tiles * LANES
    others = range(1, members)

    me = lax.axis_index("lat")
    mine_part = lax.axis_index("ens")
    core = me % 2
    side = (me // 2) % 2
    plane = me // 4

    def index_of(z, y, c):
        return (z * 2 + y) * 2 + c

    def span(c):
        return slice(c * LANES, min(nx, (c + 1) * LANES))

    def cols(c):
        return slice(c * LANES, (c + 1) * LANES)

    def copy(src, dst, ssem, rsem, to):
        return pltpu.make_async_remote_copy(
            src_ref=src, dst_ref=dst, send_sem=ssem, recv_sem=rsem, device_id=to, device_id_type=MESH
        )

    def part_span(p):
        return slice(p * part_width, min(nx, (p + 1) * part_width))

    def part_size(p):
        return part_span(p).stop - part_span(p).start

    other_side = {"lat": index_of(plane, 1 - side, core)}
    other_core = {"lat": index_of(plane, side, 1 - core)}
    above = (me + 1) % count
    below = (me + count - 1) % count
    planes = [(plane + d) % depths for d in range(1, depths)]

    barrier = pltpu.get_barrier_semaphore()
    partners = [{"lat": index_of(z, side, core)} for z in planes]
    partners += [other_side, other_core, {"lat": above}, {"lat": below}]
    partners += [{"ens": (mine_part + d) % members} for d in others]
    for partner in partners:
        pl.semaphore_signal(barrier, inc=1, device_id=partner, device_id_type=MESH)

    wet_own = ocean_ref[...].astype(jnp.float32)
    for p in range(members):
        shared[0, me, p, :, 0:part_size(p)] = depth_ref[:, part_span(p)]
        shared[1, me, p, :, 0:part_size(p)] = wet_own[:, part_span(p)]
        shared[2, me, p, :, 0:part_size(p)] = mass_ref[:, part_span(p)]
    right[me] = wet_own * surf_in[...]
    pl.semaphore_wait(barrier, len(partners))

    sent = []

    def block_of(f, index, part):
        return shared.at[f, index, part] if f < 3 else right.at[index]

    def send(ref, ssem, rsem, to):
        c = copy(ref, ref, ssem, rsem, to)
        c.start()
        sent.append(c)

    def arrived(ref, ssem, rsem):
        copy(ref, ref, ssem, rsem, other_core).wait_recv()

    for f in range(4):
        own_block = block_of(f, me, mine_part)
        for z in planes:
            send(own_block, zs.at[f, z], zr.at[f, plane], {"lat": index_of(z, side, core)})
        send(own_block, ys.at[f, plane], yr.at[f, plane], other_side)
        send(shared.at[f, me] if f < 3 else own_block, os.at[f], orx.at[f], other_core)

    for v in range(variables):
        for k in range(levels):
            up_out[pl.ds(v * levels + k, 1)] = cot_ref[v, k, block - 1:block, :]
            down_out[pl.ds(v * levels + k, 1)] = cot_ref[v, k, 0:1, :]
    for k in range(levels - 1):
        up_out[pl.ds(fields + k, 1)] = mix_ref[k, block - 1:block, :]
        down_out[pl.ds(fields + k, 1)] = mix_ref[k, 0:1, :]
    up_out[pl.ds(fields + levels - 1, 1)] = stencil_ref[4, block - 1:block, :]
    down_out[pl.ds(fields + levels - 1, 1)] = stencil_ref[3, 0:1, :]

    def ext_zero(ref):
        ref[:, :, (tiles - 1) * LANES:] = jnp.zeros(ref.shape[:2] + (LANES,), jnp.float32)
        ref[:, block:, :] = jnp.zeros((ref.shape[0], ROWS - block, width), jnp.float32)

    for ref in (cot_ext, mix_ext, coef_ext):
        ext_zero(ref)
    reverse_in[...] = jnp.zeros_like(reverse_in)
    damped = cot_ext
    for v in range(variables):
        cot_ext[pl.ds(v * levels, levels), 0:block, 0:nx] = cot_ref[v]
    mix_ext[:, 0:block, 0:nx] = mix_ref[...]
    coef_ext[:, 0:block, 0:nx] = stencil_ref[...]
    for ref in (pbuf, qbuf, rbuf):
        ref[:, :, (tiles - 1) * LANES:] = jnp.zeros((row_tiles + 2, ROWS, LANES), jnp.float32)
    xbuf[...] = jnp.zeros_like(xbuf)

    def sources(c):
        places = [(z, index_of(z, side, c)) for z in planes]
        return places + [(depths + z, index_of(z, 1 - side, c)) for z in [plane] + planes]

    def pass_on(f, k, source):
        ref = block_of(f, source, mine_part)
        send(ref, cs.at[f, k], cr.at[f, k], other_core)
        if f < 3:
            for d in others:
                send(ref, xs.at[f, d, k], xr.at[f, d, k], {"ens": (mine_part + d) % members})

    def from_planes(f):
        for z in planes:
            source = index_of(z, side, core)
            ref = block_of(f, source, mine_part)
            arrived(ref, zs.at[f, z], zr.at[f, z])
            send(ref, ys.at[f, z], yr.at[f, z], other_side)
            pass_on(f, z, source)

    def from_side(f):
        for z in [plane] + planes:
            source = index_of(z, 1 - side, core)
            arrived(block_of(f, source, mine_part), ys.at[f, z], yr.at[f, z])
            pass_on(f, depths + z, source)

    def from_members(f):
        for k, source in sources(core):
            for d in others:
                ref = shared.at[f, source, (mine_part + members - d) % members]
                arrived(ref, xs.at[f, d, k], xr.at[f, d, k])
                send(ref, fs.at[f, d, k], fr.at[f, d, k], other_core)

    def from_core(f):
        neighbour = index_of(plane, side, 1 - core)
        arrived(shared.at[f, neighbour] if f < 3 else right.at[neighbour], os.at[f], orx.at[f])
        for k, source in sources(1 - core):
            arrived(block_of(f, source, mine_part), cs.at[f, k], cr.at[f, k])
            if f < 3:
                for d in others:
                    ref = shared.at[f, source, (mine_part + members - d) % members]
                    arrived(ref, fs.at[f, d, k], fr.at[f, d, k])

    halo_up = copy(up_out, up_in, hs.at[0], hr.at[0], {"lat": above})
    halo_down = copy(down_out, down_in, hs.at[1], hr.at[1], {"lat": below})

    from_planes(0)
    from_planes(1)
    from_side(0)
    from_planes(2)
    from_side(1)
    from_members(0)
    from_planes(3)
    from_side(2)
    from_members(1)
    from_side(3)

    lane = lax.broadcasted_iota(jnp.int32, (ROWS, LANES), 1)
    sub = lax.broadcasted_iota(jnp.int32, (ROWS, LANES), 0)

    def roll(x, by):
        return pltpu.roll(x, by % LANES, 1)

    def east(get):
        first = get(0)
        now = first
        for c in range(tiles):
            if c < tiles - 1:
                after = get(c + 1)
                yield c, jnp.where(lane == LANES - 1, roll(after, -1), roll(now, -1))
                now = after
            else:
                yield c, jnp.where(lane == tail - 1, roll(first, tail - 1), roll(now, -1))

    def west(get):
        before = roll(get(tiles - 1), LANES - tail + 1)
        for c in range(tiles):
            x = get(c)
            if c == tiles - 1:
                x = jnp.where(lane < tail - 1, x, 0.0)
            rolled = roll(x, 1)
            yield c, jnp.where(lane == 0, before, rolled)
            before = rolled

    def wrap(ref):
        ref[0] = pltpu.roll(ref[row_tiles], 1, 0)
        ref[row_tiles + 1] = pltpu.roll(ref[1], ROWS - 1, 0)

    strip = row_tiles // block

    def place(t, carry, targets):
        for r in range(block):
            for field, ref in targets:
                for c in range(tiles):
                    wide = span(c).stop - span(c).start
                    p, at = c // part_tiles, c % part_tiles * LANES
                    if field < 3:
                        parts = [shared[field, s * strip + t, p, r:r + 1, at:at + wide] for s in range(ROWS)]
                    else:
                        parts = [right[s * strip + t, r:r + 1, span(c)] for s in range(ROWS)]
                    ref[t * block + r + 1, :, span(c)] = jnp.concatenate(parts, axis=0)
        return carry

    def place_all(field, ref):
        lax.fori_loop(0, strip, functools.partial(place, targets=((field, ref),)), 0)

    from_core(0)
    place_all(0, pbuf)
    from_members(2)
    from_core(1)
    halo_up.start()
    halo_down.start()
    place_all(1, qbuf)
    wrap(pbuf)
    wrap(qbuf)

    for field, ref in ((0, dbuf), (1, wbuf)):
        ref[...] = jnp.zeros_like(ref)
        for p in range(members):
            at, wide = part_span(p), part_size(p)
            ref[0:block, at] = shared[field, me, p, :, 0:wide]
            ref[block:block + 1, at] = shared[field, above, p, 0:1, 0:wide]
            ref[ROWS - 1:ROWS, at] = shared[field, below, p, block - 1:block, 0:wide]

    def links(t, carry):
        for (c, de), (_, we) in zip(east(lambda c: pbuf[t, :, cols(c)]), east(lambda c: qbuf[t, :, cols(c)])):
            d, w = pbuf[t, :, cols(c)], qbuf[t, :, cols(c)]
            ebuf[t, :, cols(c)] = 0.5 * (d + de) * w * we
            nbuf[t, :, cols(c)] = 0.5 * (d + pbuf[t + 1, :, cols(c)]) * w * qbuf[t + 1, :, cols(c)]
        return carry

    lax.fori_loop(1, row_tiles + 1, links, 0)
    for c in range(tiles):
        nbuf[row_tiles, :, cols(c)] = jnp.where(sub == ROWS - 1, 0.0, nbuf[row_tiles, :, cols(c)])
    wrap(nbuf)

    from_core(2)
    place_all(2, rbuf)

    def scales(t, carry):
        for c, ew in west(lambda c: ebuf[t, :, cols(c)]):
            centre = rbuf[t, :, cols(c)] + ebuf[t, :, cols(c)] + ew + nbuf[t, :, cols(c)] + nbuf[t - 1, :, cols(c)]
            if c == tiles - 1:
                centre = jnp.where(lane < tail, centre, 1.0)
            qbuf[t, :, cols(c)] = 1.0 / jnp.sqrt(centre)
        return carry

    lax.fori_loop(1, row_tiles + 1, scales, 0)
    wrap(qbuf)
    from_core(3)
    place_all(3, rbuf)

    def rescale(t, carry):
        for c, se in east(lambda c: qbuf[t, :, cols(c)]):
            s = qbuf[t, :, cols(c)]
            ebuf[t, :, cols(c)] = ebuf[t, :, cols(c)] * s * se
            nbuf[t, :, cols(c)] = nbuf[t, :, cols(c)] * s * qbuf[t + 1, :, cols(c)]
        return carry

    lax.fori_loop(1, row_tiles + 1, rescale, 0)
    wrap(nbuf)

    zero = jnp.zeros((ROWS, LANES), jnp.float32)

    def begin(t, acc):
        for c in range(tiles):
            r = rbuf[t, :, cols(c)] * qbuf[t, :, cols(c)]
            rbuf[t, :, cols(c)] = r
            pbuf[t, :, cols(c)] = r
            acc = acc + r * r
        return acc

    norm = jnp.sum(lax.fori_loop(1, row_tiles + 1, begin, zero))
    wrap(pbuf)
    own_tile = (me % strip) * block
    for m in range(block + 2):
        sbuf[m] = qbuf[own_tile + m]

    def iterate(_, norm):
        def apply(t, acc):
            acc = list(acc)
            for (c, pe), (_, pw) in zip(
                east(lambda c: pbuf[t, :, cols(c)]), west(lambda c: ebuf[t, :, cols(c)] * pbuf[t, :, cols(c)])
            ):
                p = pbuf[t, :, cols(c)]
                q = (p - ebuf[t, :, cols(c)] * pe - pw) - (
                    nbuf[t, :, cols(c)] * pbuf[t + 1, :, cols(c)] + nbuf[t - 1, :, cols(c)] * pbuf[t - 1, :, cols(c)]
                )
                qbuf[t, :, cols(c)] = q
                acc[c % 2] = acc[c % 2] + p * q
            return tuple(acc)

        a, b = lax.fori_loop(1, row_tiles + 1, apply, (zero, zero))
        step = norm / jnp.sum(a + b)

        def advance(m, carry):
            for c in range(tiles):
                xbuf[m, :, cols(c)] = xbuf[m, :, cols(c)] + step * pbuf[own_tile + m, :, cols(c)]
            return carry

        lax.fori_loop(0, block + 2, advance, 0)

        def residual(t, acc):
            acc = list(acc)
            for c in range(tiles):
                r = rbuf[t, :, cols(c)] - step * qbuf[t, :, cols(c)]
                rbuf[t, :, cols(c)] = r
                acc[c % 2] = acc[c % 2] + r * r
            return tuple(acc)

        a, b = lax.fori_loop(1, row_tiles + 1, residual, (zero, zero))
        new = jnp.sum(a + b)
        ratio = new / norm

        def direct(t, carry):
            for c in range(tiles):
                pbuf[t, :, cols(c)] = rbuf[t, :, cols(c)] + ratio * pbuf[t, :, cols(c)]
            return carry

        lax.fori_loop(1, row_tiles + 1, direct, 0)
        wrap(pbuf)
        return new

    lax.fori_loop(0, ITERS, iterate, norm)

    mine = jnp.where(sub == me // strip, 1.0, 0.0)
    surface_ext[...] = jnp.zeros_like(surface_ext)
    for c in range(tiles):
        for m, row in enumerate([ROWS - 1] + list(range(block + 1))):
            x = xbuf[m, :, cols(c)] * sbuf[m, :, cols(c)] * mine
            surface_ext[row:row + 1, cols(c)] = jnp.sum(x, axis=0, keepdims=True)
    surface_ref[...] = surface_ext[0:block, 0:nx]
    dbuf[...] = dbuf[...] * surface_ext[...]

    halo_up.wait()
    halo_down.wait()
    has_above = jnp.where(me < count - 1, 1.0, 0.0)
    has_below = jnp.where(me > 0, 1.0, 0.0)
    for f in range(fields):
        cot_ext[f, block:block + 1, 0:nx] = down_in[pl.ds(f, 1)]
        cot_ext[f, ROWS - 1:ROWS, 0:nx] = up_in[pl.ds(f, 1)]
    for k in range(levels - 1):
        mix_ext[k, block:block + 1, 0:nx] = down_in[pl.ds(fields + k, 1)]
        mix_ext[k, ROWS - 1:ROWS, 0:nx] = up_in[pl.ds(fields + k, 1)]
    coef_ext[3, block:block + 1, 0:nx] = down_in[pl.ds(fields + levels - 1, 1)] * has_above
    coef_ext[4, ROWS - 1:ROWS, 0:nx] = up_in[pl.ds(fields + levels - 1, 1)] * has_below

    def solve(c, carry):
        at = pl.ds(pl.multiple_of(c * LANES, LANES), LANES)
        mixes = [mix_ext[k, :, at] for k in range(levels - 1)]
        ratios, inverses = [], []
        for k in range(levels):
            under = mixes[k - 1] if k > 0 else 0.0
            over = mixes[k] if k < levels - 1 else 0.0
            pivot = 1.0 + under + over
            if k > 0:
                pivot = pivot + under * ratios[-1]
            inverse = 1.0 / pivot
            inverses.append(inverse)
            ratios.append(-over * inverse)
        lift, wet, north = dbuf[:, at], wbuf[:, at], coef_ext[4, :, at]
        for v in range(variables):
            reduced = []
            for k in range(levels):
                source = cot_ext[v * levels + k, :, at] + weights_ref[v, k] * lift
                if k > 0:
                    source = source + mixes[k - 1] * reduced[-1]
                reduced.append(source * inverses[k])
            result = reduced[-1]
            for k in range(levels - 1, -1, -1):
                if k < levels - 1:
                    result = reduced[k] - ratios[k] * result
                value = wet * result
                damped[v * levels + k, :, at] = value
                reverse_in[pl.ds(v * levels + k, 1), at] = (north * value)[block - 1:block]
        return carry

    lax.fori_loop(0, tiles, solve, 0)

    flag = jnp.where(me == count - 1, 1.0, 0.0)
    height = reverse_in.shape[0]
    a = lax.broadcasted_iota(jnp.int32, (2 * LANES, LANES), 0)
    b = lax.broadcasted_iota(jnp.int32, (2 * LANES, LANES), 1)
    permute = jnp.where(a + b == LANES + tail - 1, 1.0, 0.0)
    for c in range(tiles):
        if c < tiles - 1:
            x, m = reverse_in[:, (tiles - 2 - c) * LANES:(tiles - c) * LANES], permute
        else:
            x, m = reverse_in[:, 0:LANES], permute[LANES:]
        turned = jnp.dot(x, m, precision=lax.Precision.HIGHEST, preferred_element_type=jnp.float32)
        flipped[:, :, cols(c)] = turned[:, None, :]

    def horizontal(f, carry):
        sign = (2 * fold_ref[f // levels, f % levels] - 1).astype(jnp.float32) * flag
        for (c, pe), (_, pw) in zip(
            east(lambda c: coef_ext[1, :, cols(c)] * damped[f, :, cols(c)]),
            west(lambda c: coef_ext[2, :, cols(c)] * damped[f, :, cols(c)]),
        ):
            d = damped[f, :, cols(c)]
            value = (
                coef_ext[0, :, cols(c)] * d + pe + pw
                + pltpu.roll(coef_ext[3, :, cols(c)] * d, ROWS - 1, 0)
                + pltpu.roll(coef_ext[4, :, cols(c)] * d, 1, 0)
            )
            value = value + jnp.where(sub == block - 1, sign * flipped[f, :, cols(c)], 0.0)
            out_ref[f // levels, f % levels, :, span(c)] = value[0:block, 0:span(c).stop - span(c).start]
        return carry

    lax.fori_loop(0, fields, horizontal, 0)

    for c in sent:
        c.wait_send()


def solution(mesh):
    members, count = mesh.shape["ens"], mesh.shape["lat"]
    in_specs = (
        P("ens", None, "lat", None),
        P(("ens", "lat"), None),
        P(None, "lat", None),
        P(None, "lat", None),
        P(),
        P("lat", None),
        P("lat", None),
        P("lat", None),
        P(),
    )
    out_specs = (P("ens", None, "lat", None), P(("ens", "lat"), None))

    def shards(cot_next, cot_surface, stencil, mix, weights, depth, surface_mass, ocean, fold_sign):
        variables, levels, block, nx = cot_next.shape
        width = -(-nx // LANES) * LANES
        row_tiles = count * block // ROWS
        depths = count // 4
        part_width = -(-width // LANES // members) * LANES
        fields = variables * levels
        vmem = pl.BlockSpec(memory_space=pltpu.VMEM)
        smem = pl.BlockSpec(memory_space=pltpu.SMEM)
        f32 = jnp.float32
        ext = pltpu.VMEM((ROWS, width), f32)
        dma = pltpu.SemaphoreType.DMA
        return pl.pallas_call(
            functools.partial(kernel, members, count, block, nx, variables, levels),
            out_shape=(jax.ShapeDtypeStruct(cot_next.shape, f32), jax.ShapeDtypeStruct(cot_surface.shape, f32)),
            in_specs=[vmem, vmem, vmem, vmem, smem, vmem, vmem, vmem, smem],
            out_specs=(vmem, vmem),
            scratch_shapes=[
                pltpu.VMEM((3, count, members, block, part_width), f32),
                pltpu.VMEM((count, block, nx), f32),
                *[pltpu.VMEM((row_tiles + 2, ROWS, width), f32) for _ in range(5)],
                pltpu.VMEM((block + 2, ROWS, width), f32),
                pltpu.VMEM((block + 2, ROWS, width), f32),
                ext, ext, ext,
                pltpu.VMEM((fields, ROWS, width), f32),
                pltpu.VMEM((levels - 1, ROWS, width), f32),
                pltpu.VMEM((5, ROWS, width), f32),
                pltpu.VMEM((-(-fields // 8) * 8, 1, width), f32),
                pltpu.VMEM((-(-fields // 8) * 8, width), f32),
                *[pltpu.VMEM((fields + levels, nx), f32) for _ in range(4)],
                dma((4, depths)), dma((4, depths)), dma((4, depths)), dma((4, depths)),
                dma((4, 2 * depths)), dma((4, 2 * depths)), dma((4,)), dma((4,)),
                *[dma((3, members, 2 * depths)) for _ in range(4)], dma((2,)), dma((2,)),
            ],
            compiler_params=pltpu.CompilerParams(
                collective_id=0, has_side_effects=True, vmem_limit_bytes=60 * 1024 * 1024
            ),
        )(cot_next, cot_surface, stencil, mix, weights, depth, surface_mass, ocean, fold_sign)

    return jax.shard_map(shards, mesh=mesh, in_specs=in_specs, out_specs=out_specs, check_vma=False)
```
